32 devices in a mesh: dp: 4 (over z), tm: 4 (over y, x), space: 2 (over core).
Axes of the slice: x: 2, y: 2, z: 4, core: 2. Of those that a mesh axis runs over, the one named last changes fastest.
Arguments:
- frames: bfloat16 [4, 32, 4, 16, 512], P('dp', 'tm', 'space'), may hold values from -6 to 6
- clip_ids: int32 [4, 16], P('dp', 'tm'), may hold values from 0 to 3, never falling along the last dimension, each value on 1 to 8 neighbouring positions
- kernel: bfloat16 [3, 3, 3, 512, 512], replicated, may hold values from -0.0546875 to 0.0546875
- cotangent: bfloat16 [4, 16, 4, 16, 512], P('dp', 'tm', 'space'), may hold values from -6 to 6
Outputs:
- activated: bfloat16 [4, 16, 4, 16, 512], P('dp', 'tm', 'space')
- frame_grad: bfloat16 [4, 32, 4, 16, 512], P('dp', 'tm', 'space')
- kernel_grad: float32 [27, 262144], P(None, ('dp', 'tm', 'space'))
The draws below stay inside these ranges and needn't reach their ends.
Inputs may be any that keep to these rules, and one draw needn't show every extreme that they name: `clip_ids`: along each group's frame pairs the clip number never falls and starts at 0; each group holds 4 clips of 1 to 8 pairs, one of exactly 8 pairs.
All inputs are finite; a program needn't handle non-finite values.
Results may differ from the reference program's by a relative error of at most 0.0049.
Values may be sent and summed in bfloat16 or wider, within the bound.
A program may use at most 256 MiB of HBM per device.

```python
import math
import jax
import jax.numpy as jnp
import numpy as np
from jax import lax

C = 512
W = 16
B = 4
FO = 16
F = 32
H = 4


def with_spikes(entries, own_key, source, target, parts, factor):
    def block_of(axis_at):
        return (jnp.arange(entries.shape[axis_at]) // (entries.shape[axis_at] // parts)).reshape((-1,) + (1,) * (entries.ndim - 1 - axis_at))

    one_side = jax.random.permutation(own_key, parts)[block_of(target)]
    far = (block_of(target) + parts // 2) % parts
    return jnp.where((block_of(source) == one_side) | (block_of(source) == far), factor * entries, entries)


def steps_of(rng, shape, split, smallest, high):
    level, own = 1.0, jax.random.fold_in(rng, 6)
    for axis_at, parts in split:
        draws = jnp.exp(jax.random.uniform(jax.random.fold_in(own, axis_at), (parts,), jnp.float32, smallest / len(split), high / len(split)))
        level = level * jnp.repeat(draws, shape[axis_at] // parts).reshape([-1 if axis == axis_at else 1 for axis in range(len(shape))])
    return level


def length_profile(number_of, total, limit, skew):
    weights = [(1 << 20) // math.isqrt(standing ** skew) + 1 for standing in range(2, number_of + 1)]
    rest, counts = total - limit - (number_of - 1), [1] * (number_of - 1)
    while rest > 0:
        candidates = [i for i in range(number_of - 1) if counts[i] < limit]
        whole, left = sum([weights[i] for i in candidates]), rest
        for i in candidates:
            extra = min(limit - counts[i], max(1, left * weights[i] // whole), rest)
            counts[i] = counts[i] + extra
            rest = rest - extra
    return np.array([limit] + counts)


def uneven(rng, amount, total, limit, lean):
    if amount == 2:
        one = jax.random.randint(rng, (), max(1, total - limit), min(limit, total - 1) + 1)
        return jnp.stack([one, total - one])
    sizes = jnp.asarray(length_profile(amount, total, limit, lean), jnp.int32)
    couples = (amount - 1) // 2
    donor, sink = sizes[1:1 + 2 * couples:2], sizes[2:2 + 2 * couples:2]
    room = jnp.minimum(donor - 1, limit - sink)
    passed = jax.random.randint(jax.random.fold_in(rng, 1), (couples,), 0, 1 << 20) % (room + 1)
    sizes = sizes.at[1:1 + 2 * couples:2].set(donor - passed).at[2:2 + 2 * couples:2].set(sink + passed)
    return sizes[jax.random.permutation(jax.random.fold_in(rng, 2), amount)]


def scatter_about(rng, shape, deviation, bound, pieces=(), kind=jnp.bfloat16):
    values = deviation * jax.random.normal(rng, shape, jnp.float32)
    if pieces:
        values = values * steps_of(rng, shape, pieces, -0.22, 0.18)
    return jnp.clip(values, -bound, bound).astype(kind)


def bell_draw_with(key, dims, spread, bound, split, heavy, kind=jnp.bfloat16):
    drawn = spread * jax.random.normal(key, dims, jnp.float32)
    if split:
        drawn = drawn * steps_of(key, dims, split, -0.22, 0.18)
    return jnp.clip(with_spikes(drawn, jax.random.fold_in(key, 3), *heavy), -bound, bound).astype(kind)


def setup_inputs(seed: int = 0) -> dict:
    key_list = jax.random.split(jax.random.key(seed), 5)
    frames = bell_draw_with(key_list[0], (B, F, H, W, C), 1.0, 6.0, ((0, 4), (1, 4), (2, 2)), (1, 4, 4, 2.0))
    clip_ids = jax.vmap(lambda own: jnp.searchsorted(jnp.cumsum(uneven(own, 4, FO, FO // 2, 1)), jnp.arange(FO), side="right"))(jax.random.split(key_list[1], B)).reshape((B, FO)).astype(jnp.int32)
    kernel = scatter_about(key_list[2], (3, 3, 3, C, C), (27 * C) ** -0.5, 0.0546875)
    cotangent = scatter_about(key_list[3], (B, FO, H, W, C), 1.0, 6.0, ((0, 4), (1, 4), (2, 2)))
    return dict(frames=frames, clip_ids=clip_ids, kernel=kernel, cotangent=cotangent)


def taps_of(frames_b, link):
    count = frames_b.shape[0]
    padding = jnp.zeros((2,) + frames_b.shape[1:], frames_b.dtype)
    extended = jnp.concatenate([padding, frames_b], axis=0)
    result = []
    for time_tap in range(3):
        source = extended[time_tap:time_tap + count:2]
        if time_tap < 2:
            source = source * link[:, None, None, None]
        result.append(source)
    return result

def preact_of(frames_b, weights, link):
    total = None
    for time_tap, source in enumerate(taps_of(frames_b, link)):
        term = lax.conv_general_dilated(source, weights[time_tap], (1, 1), ((1, 1), (1, 1)), dimension_numbers=('NHWC', 'HWIO', 'NHWC'), precision=lax.Precision.HIGHEST)
        total = term if total is None else total + term
    return total

def reference(frames, clip_ids, kernel, cotangent):
    weights = kernel.astype(jnp.float32)

    def one_group(carry, item):
        frames_b, ids_b, cot_b = item
        link = jnp.concatenate([jnp.zeros((1,), jnp.float32), (ids_b[1:] == ids_b[:-1]).astype(jnp.float32)])
        preact, pullback = jax.vjp(lambda a, b: preact_of(a, b, link), frames_b.astype(jnp.float32), weights)
        gating = jax.nn.sigmoid(preact)
        activated = (preact * gating).astype(jnp.bfloat16)
        upstream = (cot_b.astype(jnp.float32) * (gating * (1.0 + preact * (1.0 - gating)))).astype(jnp.bfloat16)
        grad_frames, grad_kernel = pullback(upstream.astype(jnp.float32))
        return (carry + grad_kernel, (activated, grad_frames.astype(jnp.bfloat16)))
    total, (activated, frame_grad) = lax.scan(one_group, jnp.zeros(kernel.shape, jnp.float32), (frames, clip_ids, cotangent))
    return (activated, frame_grad, total.reshape(27, C * C))
```

```python
import jax
import jax.numpy as jnp
from jax import lax
from jax.sharding import PartitionSpec as P


def padded(array, sides, width):
    for axis, dim in sides:
        size, length = (lax.axis_size(axis), array.shape[dim])
        up = [(i, (i + 1) % size) for i in range(size - 1)]
        down = [(j, i) for i, j in up]
        last = lax.slice_in_dim(array, length - width, length, axis=dim)
        initial = lax.slice_in_dim(array, 0, width, axis=dim)
        before = lax.ppermute(last, axis, up)
        after = lax.ppermute(initial, axis, down)
        array = jnp.concatenate([before, array, after], axis=dim)
    return array


def from_behind(value, axis, steps):
    count = lax.axis_size(axis)
    initial, last = (max(0, -steps), min(count, count - steps))
    return lax.ppermute(value, axis, [(source, source + steps) for source in range(initial, last)])


def widen_columns(field):
    return jnp.pad(field, ((0, 0), (0, 0), (0, 0), (1, 1), (0, 0)))


AXES = ("dp", "tm", "space")


def patches_of_own_channels(frames, clip_ids):
    dp, tm, space = (lax.axis_size(axis) for axis in AXES)
    count = dp * tm * space
    groups, steps, height, columns, channels = frames.shape
    pairs = clip_ids.shape[1]
    own = channels // count
    sent = frames.reshape(-1, count, own).transpose(1, 0, 2)
    got = lax.all_to_all(sent, AXES, 0, 0)
    got = got.reshape(dp, tm, space, groups, steps, height, columns, own)
    whole = got.transpose(0, 3, 7, 1, 4, 2, 5, 6).reshape(
        dp * groups, own, tm * steps, space * height, columns
    )
    ids = lax.all_gather(clip_ids, "dp", axis=0, tiled=True)
    ids = lax.all_gather(ids, "tm", axis=1, tiled=True)
    linked = jnp.pad(ids[:, 1:] == ids[:, :-1], ((0, 0), (1, 0))).astype(jnp.bfloat16)
    linked = linked[:, None, :, None, None]
    wide = jnp.pad(whole, ((0, 0), (0, 0), (2, 0), (1, 1), (1, 1)))
    rows = []
    for time_tap in range(3):
        source = wide[:, :, time_tap : time_tap + tm * steps : 2]
        if time_tap < 2:
            source = source * linked
        for row_tap in range(3):
            for col_tap in range(3):
                rows.append(
                    source[
                        :, :, :, row_tap : row_tap + space * height, col_tap : col_tap + columns
                    ]
                )
    field = jnp.stack(rows, axis=0).reshape(
        27, dp, groups, own, tm, pairs, space, height, columns
    )
    return field.transpose(0, 3, 1, 4, 6, 2, 5, 7, 8).reshape(27 * own, -1)


def weight_grad(patches, upstream):
    gathered = lax.all_gather(upstream, AXES, axis=0, tiled=True)
    grad = jnp.dot(patches, gathered, preferred_element_type=jnp.float32)
    return grad.reshape(27, -1)


def per_device(frames, clip_ids, kernel, cotangent):
    pair_count = clip_ids.shape[1]
    height = frames.shape[2]
    columns = frames.shape[3]
    channels = frames.shape[4]
    cell_count = pair_count * height * columns
    channel_patches = patches_of_own_channels(frames, clip_ids)
    rowed = padded(frames, (("space", 2),), 1)
    earlier, prior_id = from_behind((rowed[:, -2:], clip_ids[:, -1:]), "tm", 1)
    extended = widen_columns(jnp.concatenate([earlier, rowed], axis=1))
    linked = (jnp.concatenate([prior_id, clip_ids[:, :-1]], axis=1) == clip_ids).astype(
        jnp.bfloat16
    )
    linked = linked[:, :, None, None, None]
    preact = jnp.zeros((cell_count, channels), jnp.float32)
    for time_tap in range(3):
        source = extended[:, time_tap : time_tap + 2 * pair_count : 2]
        if time_tap < 2:
            source = source * linked
        for row_tap in range(3):
            row_band = source[:, :, row_tap : row_tap + height]
            block = jnp.concatenate(
                [row_band[:, :, :, col_tap : col_tap + columns] for col_tap in range(3)], axis=-1
            ).reshape(cell_count, 3 * channels)
            preact = preact + jnp.dot(
                block,
                kernel[time_tap, row_tap].reshape(3 * channels, channels),
                preferred_element_type=jnp.float32,
            )
    gating = jax.nn.sigmoid(preact)
    grid_shape = (frames.shape[0], pair_count, height, columns, channels)
    activated = (preact * gating).astype(jnp.bfloat16).reshape(grid_shape)
    upstream = (
        cotangent.reshape(cell_count, channels).astype(jnp.float32)
        * (gating * (1.0 + preact * (1.0 - gating)))
    ).astype(jnp.bfloat16)
    kernel_grad = weight_grad(channel_patches, upstream)
    grid = upstream.reshape(grid_shape)
    padded_rows = padded(grid, (("space", 2),), 1)
    later, next_id = from_behind((padded_rows[:, :1], clip_ids[:, :1]), "tm", -1)
    following = jnp.concatenate([padded_rows[:, 1:], later], axis=1)
    onward = (jnp.concatenate([clip_ids[:, 1:], next_id], axis=1) == clip_ids).astype(jnp.bfloat16)
    following = widen_columns(following * onward[:, :, None, None, None])
    current = widen_columns(padded_rows)

    def transpose_conv(field, time_tap):
        total = jnp.zeros((cell_count, channels), jnp.float32)
        for row_tap in range(3):
            row_band = field[:, :, 2 - row_tap : 2 - row_tap + height]
            stacked = jnp.stack(
                [row_band[:, :, :, 2 - col_tap : 2 - col_tap + columns] for col_tap in range(3)],
                axis=-2,
            ).reshape(cell_count, 3, channels)
            total = total + lax.dot_general(
                stacked,
                kernel[time_tap, row_tap],
                (((1, 2), (0, 2)), ((), ())),
                preferred_element_type=jnp.float32,
            )
        return total

    even_grad = transpose_conv(current, 2) + transpose_conv(following, 0)
    odd_grad = transpose_conv(following, 1)
    frame_grad = jnp.stack([even_grad.reshape(grid_shape), odd_grad.reshape(grid_shape)], axis=2)
    frame_grad = frame_grad.reshape(frames.shape).astype(jnp.bfloat16)
    return (activated, frame_grad, kernel_grad)


def solution(mesh):
    return jax.shard_map(
        per_device,
        mesh=mesh,
        in_specs=(
            P("dp", "tm", "space", None, None),
            P("dp", "tm"),
            P(),
            P("dp", "tm", "space", None, None),
        ),
        out_specs=(
            P("dp", "tm", "space", None, None),
            P("dp", "tm", "space", None, None),
            P(None, ("dp", "tm", "space")),
        ),
        check_vma=False,
    )
```

```python
import functools

import jax
import jax.numpy as jnp
from jax import lax
from jax.experimental import pallas as pl
from jax.experimental.pallas import tpu as pltpu
from jax.sharding import PartitionSpec as P

AXES = ("dp", "tm", "space")
VMEM_BYTES = 48 * 2**20


def row_halo(array):
    size = lax.axis_size("space")
    up = [(i, i + 1) for i in range(size - 1)]
    down = [(i + 1, i) for i in range(size - 1)]
    before = lax.ppermute(array[:, :, -1:], "space", up)
    after = lax.ppermute(array[:, :, :1], "space", down)
    return jnp.concatenate([before, array, after], axis=2)


def from_behind(value, steps):
    count = lax.axis_size("tm")
    first, last = max(0, -steps), min(count, count - steps)
    return lax.ppermute(value, "tm", [(i, i + steps) for i in range(first, last)])


def column_taps(base, columns):
    count = base.shape[0]
    wide = base.astype(jnp.float32)
    column = lax.broadcasted_iota(jnp.int32, base.shape, 0) % columns
    left = jnp.where(column > 0, pltpu.roll(wide, 1, 0), 0.0)
    right = jnp.where(column < columns - 1, pltpu.roll(wide, count - 1, 0), 0.0)
    return left.astype(base.dtype), base, right.astype(base.dtype)


def forward_body(columns, height, planes, weights, cotangent, activated, upstream, total):
    step = pl.program_id(0)
    time_tap, row_tap = step // 3, step % 3
    pairs, channels = planes.shape[1], planes.shape[-1]
    base = planes[time_tap, :, pl.ds(row_tap, height)].reshape(pairs * height * columns, channels)
    block = jnp.concatenate(column_taps(base, columns), axis=1)
    term = jnp.dot(
        block,
        weights[0, 0].reshape(3 * channels, channels),
        preferred_element_type=jnp.float32,
    )

    @pl.when(step == 0)
    def _():
        total[...] = term

    @pl.when(step > 0)
    def _():
        total[...] += term

    @pl.when(step == 8)
    def _():
        preact = total[...]
        gating = jax.nn.sigmoid(preact)
        activated[...] = (preact * gating).astype(activated.dtype)
        slope = gating * (1.0 + preact * (1.0 - gating))
        upstream[...] = (cotangent[...].astype(jnp.float32) * slope).astype(upstream.dtype)


def backward_body(columns, height, fields, weights, out, total):
    step = pl.program_id(0)
    place, row_tap = step // 3, step % 3
    pairs, channels = fields.shape[1], fields.shape[-1]
    source = jnp.where(place == 1, 1, 0)
    base = fields[source, :, pl.ds(2 - row_tap, height)].reshape(
        pairs * height * columns, channels
    )
    left, middle, right = column_taps(base, columns)
    term = None
    for col_tap, part in enumerate((right, middle, left)):
        product = lax.dot_general(
            part,
            weights[0, 0, col_tap],
            (((1,), (1,)), ((), ())),
            preferred_element_type=jnp.float32,
        )
        term = product if term is None else term + product
    fresh = (step == 0) | (step == 6)

    @pl.when(fresh)
    def _():
        total[...] = term

    @pl.when(jnp.logical_not(fresh))
    def _():
        total[...] += term

    def store(parity):
        value = total[...].astype(out.dtype)
        out[:, parity] = value.reshape(pairs, height * columns, channels)

    @pl.when(step == 5)
    def _():
        store(0)

    @pl.when(step == 8)
    def _():
        store(1)


def weight_body(columns, rows, planes, upstream, out):
    cells = planes.shape[-1]
    own = planes.shape[-2]
    lane = lax.broadcasted_iota(jnp.int32, (own, cells), 1)
    column = lane % columns
    row = (lane // columns) % rows
    frame = rows * columns
    parts = []
    for time_tap in range(3):
        plane = planes[0, 0, time_tap].astype(jnp.float32)
        if time_tap < 2:
            plane = jnp.where(lane >= frame, pltpu.roll(plane, frame, 1), 0.0)
        for down in (-1, 0, 1):
            for right in (-1, 0, 1):
                shift = down * columns + right
                moved = pltpu.roll(plane, (-shift) % cells, 1) if shift else plane
                inside = (row + down >= 0) & (row + down < rows)
                inside = inside & (column + right >= 0) & (column + right < columns)
                parts.append(jnp.where(inside, moved, 0.0))
    patches = jnp.concatenate(parts, axis=0).astype(jnp.bfloat16)
    _, tm, space, _, pairs, _, _ = upstream.shape
    field = jnp.concatenate(
        [upstream[0, t, s, 0, p] for t in range(tm) for p in range(pairs) for s in range(space)],
        axis=0,
    )
    term = jnp.dot(patches, field, preferred_element_type=jnp.float32)
    first = (pl.program_id(0) == 0) & (pl.program_id(1) == 0)

    @pl.when(first)
    def _():
        out[...] = term

    @pl.when(jnp.logical_not(first))
    def _():
        out[...] += term


def per_device(frames, clip_ids, kernel, cotangent):
    dp, tm, space = (lax.axis_size(axis) for axis in AXES)
    groups, steps, height, columns, channels = frames.shape
    pairs = clip_ids.shape[1]
    slots = groups * pairs
    frame = height * columns
    cells = slots * frame
    own = channels // (dp * tm * space)
    bf16 = jnp.bfloat16

    next_id = from_behind(clip_ids[:, :1], -1)
    prior_id = from_behind(clip_ids[:, -1:], 1)
    linked = (jnp.concatenate([prior_id, clip_ids[:, :-1]], axis=1) == clip_ids).astype(bf16)
    onward = (jnp.concatenate([clip_ids[:, 1:], next_id], axis=1) == clip_ids).astype(bf16)

    paired = frames.reshape(slots, 2, frame, channels)
    kept = onward.reshape(slots, 1, 1)
    even, odd = paired[:, 0], paired[:, 1]
    planes = jnp.stack([even * kept, odd * kept, even], axis=0).reshape(3 * cells, channels)
    sent = planes.T.reshape(dp * tm * space, own, 3 * cells)
    got = lax.all_to_all(sent, AXES, 0, 0)
    got = got.reshape(dp, tm, space, own, 3, groups, pairs, frame)
    own_planes = got.transpose(0, 5, 4, 3, 1, 6, 2, 7).reshape(dp, groups, 3, own, -1)

    rowed = row_halo(frames)
    earlier = from_behind(rowed[:, -2:], 1)
    extended = jnp.concatenate([earlier, rowed], axis=1)
    gate = linked[:, :, None, None, None]
    taps = jnp.stack(
        [
            extended[:, 0 : 2 * pairs : 2] * gate,
            extended[:, 1 : 1 + 2 * pairs : 2] * gate,
            extended[:, 2 : 2 + 2 * pairs : 2],
        ],
        axis=0,
    ).reshape(3, slots, height + 2, columns, channels)

    whole = pl.BlockSpec(memory_space=pltpu.VMEM)
    params = pltpu.CompilerParams(vmem_limit_bytes=VMEM_BYTES)
    flops = 2 * 27 * cells * channels * channels
    weight_bytes = 27 * channels * channels * 2
    cost = pl.CostEstimate(flops=flops, bytes_accessed=weight_bytes, transcendentals=0)
    flat = jax.ShapeDtypeStruct((cells, channels), bf16)
    activated, upstream = pl.pallas_call(
        functools.partial(forward_body, columns, height),
        grid=(9,),
        out_shape=(flat, flat),
        in_specs=[
            whole,
            pl.BlockSpec((1, 1, 3, channels, channels), lambda i: (i // 3, i % 3, 0, 0, 0)),
            whole,
        ],
        out_specs=(
            pl.BlockSpec((cells, channels), lambda i: (0, 0)),
            pl.BlockSpec((cells, channels), lambda i: (0, 0)),
        ),
        scratch_shapes=[pltpu.VMEM((cells, channels), jnp.float32)],
        compiler_params=params,
        cost_estimate=cost,
    )(taps, kernel, cotangent.reshape(cells, channels))

    gathered = lax.all_gather(upstream, AXES, axis=0, tiled=True)

    grid = upstream.reshape(groups, pairs, height, columns, channels)
    padded = row_halo(grid)
    later = from_behind(padded[:, :1], -1)
    following = jnp.concatenate([padded[:, 1:], later], axis=1)
    following = following * onward[:, :, None, None, None]
    fields = jnp.stack([following, padded], axis=0).reshape(
        2, slots, height + 2, columns, channels
    )
    frame_grad = pl.pallas_call(
        functools.partial(backward_body, columns, height),
        grid=(9,),
        out_shape=jax.ShapeDtypeStruct((slots, 2, frame, channels), bf16),
        in_specs=[
            whole,
            pl.BlockSpec(
                (1, 1, 3, channels, channels), lambda i: ((i // 3) * 2 % 3, i % 3, 0, 0, 0)
            ),
        ],
        out_specs=pl.BlockSpec((slots, 2, frame, channels), lambda i: (0, 0, 0, 0)),
        scratch_shapes=[pltpu.VMEM((cells, channels), jnp.float32)],
        compiler_params=params,
        cost_estimate=cost,
    )(fields, kernel)

    per_group = gathered.reshape(dp, tm, space, groups, pairs, frame, channels)
    group_cells = tm * pairs * space * frame
    kernel_grad = pl.pallas_call(
        functools.partial(weight_body, columns, space * height),
        grid=(dp, groups),
        out_shape=jax.ShapeDtypeStruct((27 * own, channels), jnp.float32),
        in_specs=[
            pl.BlockSpec((1, 1, 3, own, group_cells), lambda a, b: (a, b, 0, 0, 0)),
            pl.BlockSpec(
                (1, tm, space, 1, pairs, frame, channels), lambda a, b: (a, 0, 0, b, 0, 0, 0)
            ),
        ],
        out_specs=pl.BlockSpec((27 * own, channels), lambda a, b: (0, 0)),
        compiler_params=params,
        cost_estimate=pl.CostEstimate(
            flops=flops, bytes_accessed=2 * gathered.size, transcendentals=0
        ),
    )(own_planes, per_group)

    return (
        activated.reshape(cotangent.shape),
        frame_grad.reshape(frames.shape),
        kernel_grad.reshape(27, own * channels),
    )


def solution(mesh):
    return jax.shard_map(
        per_device,
        mesh=mesh,
        in_specs=(
            P("dp", "tm", "space", None, None),
            P("dp", "tm"),
            P(),
            P("dp", "tm", "space", None, None),
        ),
        out_specs=(
            P("dp", "tm", "space", None, None),
            P("dp", "tm", "space", None, None),
            P(None, ("dp", "tm", "space")),
        ),
        check_vma=False,
    )
```

```python
import functools

import jax
import jax.numpy as jnp
from jax import lax
from jax.experimental import pallas as pl
from jax.experimental.pallas import tpu as pltpu
from jax.sharding import PartitionSpec as P

AXES = ("dp", "tm", "space")
VMEM_BYTES = 48 * 2**20


def row_halo(array):
    size = lax.axis_size("space")
    up = [(i, i + 1) for i in range(size - 1)]
    down = [(i + 1, i) for i in range(size - 1)]
    before = lax.ppermute(array[:, :, -1:], "space", up)
    after = lax.ppermute(array[:, :, :1], "space", down)
    return jnp.concatenate([before, array, after], axis=2)


def from_behind(value, steps):
    count = lax.axis_size("tm")
    first, last = max(0, -steps), min(count, count - steps)
    return lax.ppermute(value, "tm", [(i, i + steps) for i in range(first, last)])


def column_taps(base, columns):
    count = base.shape[0]
    wide = base.astype(jnp.float32)
    column = lax.broadcasted_iota(jnp.int32, base.shape, 0) % columns
    left = jnp.where(column > 0, pltpu.roll(wide, 1, 0), 0.0)
    right = jnp.where(column < columns - 1, pltpu.roll(wide, count - 1, 0), 0.0)
    return left.astype(base.dtype), base, right.astype(base.dtype)


def forward_body(columns, height, planes, weights, cotangent, activated, upstream, total):
    step = pl.program_id(0)
    time_tap, row_tap = step // 3, step % 3
    pairs, channels = planes.shape[1], planes.shape[-1]
    base = planes[time_tap, :, pl.ds(row_tap, height)].reshape(pairs * height * columns, channels)
    block = jnp.concatenate(column_taps(base, columns), axis=1)
    term = jnp.dot(
        block,
        weights[0, 0].reshape(3 * channels, channels),
        preferred_element_type=jnp.float32,
    )

    @pl.when(step == 0)
    def _():
        total[...] = term

    @pl.when(step > 0)
    def _():
        total[...] += term

    @pl.when(step == 8)
    def _():
        preact = total[...]
        gating = jax.nn.sigmoid(preact)
        activated[...] = (preact * gating).astype(activated.dtype)
        slope = gating * (1.0 + preact * (1.0 - gating))
        upstream[...] = (cotangent[...].astype(jnp.float32) * slope).astype(upstream.dtype)


def gather_parts(upstream, everyone, own_sem, send_sems, recv_sems):
    here = {axis: lax.axis_index(axis) for axis in AXES}
    size = {axis: lax.axis_size(axis) for axis in AXES}
    dp, tm, space = (size[axis] for axis in AXES)
    peers = {
        axis: [lax.rem(here[axis] + k, size[axis]) for k in range(1, size[axis])] for axis in AXES
    }

    def flat(s, t, d):
        return (s * tm + t) * dp + d

    def copy(source, block, number, axis, target):
        index = flat(*block)
        return pltpu.make_async_remote_copy(
            src_ref=upstream if source is None else everyone.at[index],
            dst_ref=everyone.at[index],
            send_sem=send_sems.at[number],
            recv_sem=recv_sems.at[index],
            device_id={axis: target},
            device_id_type=pl.DeviceIdType.MESH,
        )

    mine = (here["space"], here["tm"], here["dp"])
    column = [(here["space"], here["tm"], d) for d in peers["dp"]]
    plane = [
        (here["space"], t, d) for t in peers["tm"] for d in [here["dp"]] + peers["dp"]
    ]
    far = [
        (s, t, d)
        for s in peers["space"]
        for t in [here["tm"]] + peers["tm"]
        for d in [here["dp"]] + peers["dp"]
    ]
    plan, stages = [], []
    stages.append([(None, mine, axis, p) for axis in AXES for p in peers[axis]])
    stages.append([(1, b, axis, p) for b in column for axis in AXES[1:] for p in peers[axis]])
    stages.append([(1, b, "space", p) for b in plane for p in peers["space"]])
    number = 0
    for stage in stages:
        row = []
        for source, block, axis, target in stage:
            row.append(copy(source, block, number, axis, target))
            number += 1
        plan.append(row)
    keep = pltpu.make_async_copy(upstream, everyone.at[flat(*mine)], own_sem)

    def arrived(blocks):
        for block in blocks:
            copy(1, block, 0, "dp", peers["dp"][0]).wait_recv()

    def begin():
        barrier = pltpu.get_barrier_semaphore()
        for axis in AXES:
            for p in peers[axis]:
                pl.semaphore_signal(
                    barrier, inc=1, device_id={axis: p}, device_id_type=pl.DeviceIdType.MESH
                )
        pl.semaphore_wait(barrier, dp + tm + space - 3)
        for one in plan[0]:
            one.start()
        keep.start()

    def middle():
        per_block = len(plan[1]) // len(column)
        for k, block in enumerate(column):
            arrived([block])
            for one in plan[1][k * per_block : (k + 1) * per_block]:
                one.start()

    def finish():
        per_block = len(plan[2]) // len(plane)
        for k, block in enumerate(plane):
            arrived([block])
            for one in plan[2][k * per_block : (k + 1) * per_block]:
                one.start()
        arrived(far)
        keep.wait()
        for row in plan:
            for one in row:
                one.wait_send()

    return begin, middle, finish


def backward_body(
    columns,
    height,
    fields,
    weights,
    upstream,
    out,
    everyone,
    total,
    own_sem,
    send_sems,
    recv_sems,
):
    step = pl.program_id(0)
    begin, middle, finish = gather_parts(upstream, everyone, own_sem, send_sems, recv_sems)
    pl.when(step == 0)(begin)
    pl.when(step == 4)(middle)
    place, row_tap = step // 3, step % 3
    pairs, channels = fields.shape[1], fields.shape[-1]
    source = jnp.where(place == 1, 1, 0)
    base = fields[source, :, pl.ds(2 - row_tap, height)].reshape(
        pairs * height * columns, channels
    )
    left, middle, right = column_taps(base, columns)
    term = None
    for col_tap, part in enumerate((right, middle, left)):
        product = lax.dot_general(
            part,
            weights[0, 0, col_tap],
            (((1,), (1,)), ((), ())),
            preferred_element_type=jnp.float32,
        )
        term = product if term is None else term + product
    fresh = (step == 0) | (step == 6)

    @pl.when(fresh)
    def _():
        total[...] = term

    @pl.when(jnp.logical_not(fresh))
    def _():
        total[...] += term

    def store(parity):
        value = total[...].astype(out.dtype)
        out[:, parity] = value.reshape(pairs, height * columns, channels)

    @pl.when(step == 5)
    def _():
        store(0)

    @pl.when(step == 8)
    def _():
        store(1)
        finish()


def weight_body(columns, rows, planes, upstream, out):
    cells = planes.shape[-1]
    own = planes.shape[-2]
    lane = lax.broadcasted_iota(jnp.int32, (own, cells), 1)
    column = lane % columns
    row = (lane // columns) % rows
    frame = rows * columns
    parts = []
    for time_tap in range(3):
        plane = planes[0, 0, time_tap].astype(jnp.float32)
        if time_tap < 2:
            plane = jnp.where(lane >= frame, pltpu.roll(plane, frame, 1), 0.0)
        for down in (-1, 0, 1):
            for right in (-1, 0, 1):
                shift = down * columns + right
                moved = pltpu.roll(plane, (-shift) % cells, 1) if shift else plane
                inside = (row + down >= 0) & (row + down < rows)
                inside = inside & (column + right >= 0) & (column + right < columns)
                parts.append(jnp.where(inside, moved, 0.0))
    patches = jnp.concatenate(parts, axis=0).astype(jnp.bfloat16)
    space, tm, _, _, pairs, _, _ = upstream.shape
    field = jnp.concatenate(
        [upstream[s, t, 0, 0, p] for t in range(tm) for p in range(pairs) for s in range(space)],
        axis=0,
    )
    term = jnp.dot(patches, field, preferred_element_type=jnp.float32)
    first = (pl.program_id(0) == 0) & (pl.program_id(1) == 0)

    @pl.when(first)
    def _():
        out[...] = term

    @pl.when(jnp.logical_not(first))
    def _():
        out[...] += term


def per_device(frames, clip_ids, kernel, cotangent):
    dp, tm, space = (lax.axis_size(axis) for axis in AXES)
    groups, steps, height, columns, channels = frames.shape
    pairs = clip_ids.shape[1]
    slots = groups * pairs
    frame = height * columns
    cells = slots * frame
    own = channels // (dp * tm * space)
    bf16 = jnp.bfloat16

    next_id = from_behind(clip_ids[:, :1], -1)
    prior_id = from_behind(clip_ids[:, -1:], 1)
    linked = (jnp.concatenate([prior_id, clip_ids[:, :-1]], axis=1) == clip_ids).astype(bf16)
    onward = (jnp.concatenate([clip_ids[:, 1:], next_id], axis=1) == clip_ids).astype(bf16)

    paired = frames.reshape(slots, 2, frame, channels)
    kept = onward.reshape(slots, 1, 1)
    even, odd = paired[:, 0], paired[:, 1]
    planes = jnp.stack([even * kept, odd * kept, even], axis=0).reshape(3 * cells, channels)
    sent = planes.T.reshape(dp * tm * space, own, 3 * cells)
    got = lax.all_to_all(sent, AXES, 0, 0)
    got = got.reshape(dp, tm, space, own, 3, groups, pairs, frame)
    own_planes = got.transpose(0, 5, 4, 3, 1, 6, 2, 7).reshape(dp, groups, 3, own, -1)

    rowed = row_halo(frames)
    earlier = from_behind(rowed[:, -2:], 1)
    extended = jnp.concatenate([earlier, rowed], axis=1)
    gate = linked[:, :, None, None, None]
    taps = jnp.stack(
        [
            extended[:, 0 : 2 * pairs : 2] * gate,
            extended[:, 1 : 1 + 2 * pairs : 2] * gate,
            extended[:, 2 : 2 + 2 * pairs : 2],
        ],
        axis=0,
    ).reshape(3, slots, height + 2, columns, channels)

    whole = pl.BlockSpec(memory_space=pltpu.VMEM)
    params = pltpu.CompilerParams(vmem_limit_bytes=VMEM_BYTES)
    flops = 2 * 27 * cells * channels * channels
    weight_bytes = 27 * channels * channels * 2
    cost = pl.CostEstimate(flops=flops, bytes_accessed=weight_bytes, transcendentals=0)
    flat = jax.ShapeDtypeStruct((cells, channels), bf16)
    activated, upstream = pl.pallas_call(
        functools.partial(forward_body, columns, height),
        grid=(9,),
        out_shape=(flat, flat),
        in_specs=[
            whole,
            pl.BlockSpec((1, 1, 3, channels, channels), lambda i: (i // 3, i % 3, 0, 0, 0)),
            whole,
        ],
        out_specs=(
            pl.BlockSpec((cells, channels), lambda i: (0, 0)),
            pl.BlockSpec((cells, channels), lambda i: (0, 0)),
        ),
        scratch_shapes=[pltpu.VMEM((cells, channels), jnp.float32)],
        compiler_params=params,
        cost_estimate=cost,
    )(taps, kernel, cotangent.reshape(cells, channels))

    count = dp * tm * space
    grid = upstream.reshape(groups, pairs, height, columns, channels)
    padded = row_halo(grid)
    later = from_behind(padded[:, :1], -1)
    following = jnp.concatenate([padded[:, 1:], later], axis=1)
    following = following * onward[:, :, None, None, None]
    fields = jnp.stack([following, padded], axis=0).reshape(
        2, slots, height + 2, columns, channels
    )
    frame_grad, gathered = pl.pallas_call(
        functools.partial(backward_body, columns, height),
        grid=(9,),
        out_shape=(
            jax.ShapeDtypeStruct((slots, 2, frame, channels), bf16),
            jax.ShapeDtypeStruct((count, cells, channels), bf16),
        ),
        in_specs=[
            whole,
            pl.BlockSpec(
                (1, 1, 3, channels, channels), lambda i: ((i // 3) * 2 % 3, i % 3, 0, 0, 0)
            ),
            pl.BlockSpec(memory_space=pl.ANY),
        ],
        out_specs=(
            pl.BlockSpec((slots, 2, frame, channels), lambda i: (0, 0, 0, 0)),
            pl.BlockSpec(memory_space=pl.ANY),
        ),
        scratch_shapes=[
            pltpu.VMEM((cells, channels), jnp.float32),
            pltpu.SemaphoreType.DMA,
            pltpu.SemaphoreType.DMA((count - 1,)),
            pltpu.SemaphoreType.DMA((count,)),
        ],
        compiler_params=pltpu.CompilerParams(
            vmem_limit_bytes=VMEM_BYTES, collective_id=0, has_side_effects=True
        ),
        cost_estimate=cost,
    )(fields, kernel, upstream)

    per_group = gathered.reshape(space, tm, dp, groups, pairs, frame, channels)
    group_cells = tm * pairs * space * frame
    kernel_grad = pl.pallas_call(
        functools.partial(weight_body, columns, space * height),
        grid=(dp, groups),
        out_shape=jax.ShapeDtypeStruct((27 * own, channels), jnp.float32),
        in_specs=[
            pl.BlockSpec((1, 1, 3, own, group_cells), lambda a, b: (a, b, 0, 0, 0)),
            pl.BlockSpec(
                (space, tm, 1, 1, pairs, frame, channels), lambda a, b: (0, 0, a, b, 0, 0, 0)
            ),
        ],
        out_specs=pl.BlockSpec((27 * own, channels), lambda a, b: (0, 0)),
        compiler_params=params,
        cost_estimate=pl.CostEstimate(
            flops=flops, bytes_accessed=2 * gathered.size, transcendentals=0
        ),
    )(own_planes, per_group)

    return (
        activated.reshape(cotangent.shape),
        frame_grad.reshape(frames.shape),
        kernel_grad.reshape(27, own * channels),
    )


def solution(mesh):
    return jax.shard_map(
        per_device,
        mesh=mesh,
        in_specs=(
            P("dp", "tm", "space", None, None),
            P("dp", "tm"),
            P(),
            P("dp", "tm", "space", None, None),
        ),
        out_specs=(
            P("dp", "tm", "space", None, None),
            P("dp", "tm", "space", None, None),
            P(None, ("dp", "tm", "space")),
        ),
        check_vma=False,
    )
```

```python
import functools

import jax
import jax.numpy as jnp
from jax import lax
from jax.experimental import pallas as pl
from jax.experimental.pallas import tpu as pltpu
from jax.sharding import PartitionSpec as P

AXES = ("dp", "tm", "space")
VMEM_BYTES = 48 * 2**20


def row_halo(array):
    size = lax.axis_size("space")
    up = [(i, i + 1) for i in range(size - 1)]
    down = [(i + 1, i) for i in range(size - 1)]
    before = lax.ppermute(array[:, :, -1:], "space", up)
    after = lax.ppermute(array[:, :, :1], "space", down)
    return jnp.concatenate([before, array, after], axis=2)


def from_behind(value, steps):
    count = lax.axis_size("tm")
    first, last = max(0, -steps), min(count, count - steps)
    return lax.ppermute(value, "tm", [(i, i + steps) for i in range(first, last)])


def haloed_from_behind(value, steps):
    count, size = lax.axis_size("tm"), lax.axis_size("space")

    def edge(rows, move):
        perm = [
            (t * size + s, (t + steps) * size + s + move)
            for t in range(max(0, -steps), min(count, count - steps))
            for s in range(max(0, -move), min(size, size - move))
        ]
        return lax.ppermute(rows, ("tm", "space"), perm)

    middle = from_behind(value, steps)
    before = edge(value[:, :, -1:], 1)
    after = edge(value[:, :, :1], -1)
    return jnp.concatenate([before, middle, after], axis=2)


def column_taps(base, columns):
    count = base.shape[0]
    wide = base.astype(jnp.float32)
    column = lax.broadcasted_iota(jnp.int32, base.shape, 0) % columns
    left = jnp.where(column > 0, pltpu.roll(wide, 1, 0), 0.0)
    right = jnp.where(column < columns - 1, pltpu.roll(wide, count - 1, 0), 0.0)
    return left.astype(base.dtype), base, right.astype(base.dtype)


def forward_body(columns, height, planes, weights, cotangent, activated, upstream, total):
    step = pl.program_id(0)
    time_tap, row_tap = step // 3, step % 3
    pairs, channels = planes.shape[1], planes.shape[-1]
    base = planes[time_tap, :, pl.ds(row_tap, height)].reshape(pairs * height * columns, channels)
    block = jnp.concatenate(column_taps(base, columns), axis=1)
    term = jnp.dot(
        block,
        weights[0, 0].reshape(3 * channels, channels),
        preferred_element_type=jnp.float32,
    )

    @pl.when(step == 0)
    def _():
        total[...] = term

    @pl.when(step > 0)
    def _():
        total[...] += term

    @pl.when(step == 8)
    def _():
        preact = total[...]
        gating = jax.nn.sigmoid(preact)
        activated[...] = (preact * gating).astype(activated.dtype)
        slope = gating * (1.0 + preact * (1.0 - gating))
        upstream[...] = (cotangent[...].astype(jnp.float32) * slope).astype(upstream.dtype)


def gather_parts(upstream, everyone, own_sem, send_sems, recv_sems):
    here = {axis: lax.axis_index(axis) for axis in AXES}
    size = {axis: lax.axis_size(axis) for axis in AXES}
    dp, tm, space = (size[axis] for axis in AXES)
    peers = {
        axis: [lax.rem(here[axis] + k, size[axis]) for k in range(1, size[axis])] for axis in AXES
    }

    def flat(s, t, d):
        return (s * tm + t) * dp + d

    def copy(source, block, number, axis, target):
        index = flat(*block)
        return pltpu.make_async_remote_copy(
            src_ref=upstream if source is None else everyone.at[index],
            dst_ref=everyone.at[index],
            send_sem=send_sems.at[number],
            recv_sem=recv_sems.at[index],
            device_id={axis: target},
            device_id_type=pl.DeviceIdType.MESH,
        )

    mine = (here["space"], here["tm"], here["dp"])
    column = [(here["space"], here["tm"], d) for d in peers["dp"]]
    plane = [
        (here["space"], t, d) for t in peers["tm"] for d in [here["dp"]] + peers["dp"]
    ]
    far = [
        (s, t, d)
        for s in peers["space"]
        for t in [here["tm"]] + peers["tm"]
        for d in [here["dp"]] + peers["dp"]
    ]
    plan, stages = [], []
    stages.append([(None, mine, axis, p) for axis in AXES for p in peers[axis]])
    stages.append([(1, b, axis, p) for b in column for axis in AXES[1:] for p in peers[axis]])
    stages.append([(1, b, "space", p) for b in plane for p in peers["space"]])
    number = 0
    for stage in stages:
        row = []
        for source, block, axis, target in stage:
            row.append(copy(source, block, number, axis, target))
            number += 1
        plan.append(row)
    keep = pltpu.make_async_copy(upstream, everyone.at[flat(*mine)], own_sem)

    def arrived(blocks):
        for block in blocks:
            copy(1, block, 0, "dp", peers["dp"][0]).wait_recv()

    def begin():
        barrier = pltpu.get_barrier_semaphore()
        for axis in AXES:
            for p in peers[axis]:
                pl.semaphore_signal(
                    barrier, inc=1, device_id={axis: p}, device_id_type=pl.DeviceIdType.MESH
                )
        pl.semaphore_wait(barrier, dp + tm + space - 3)
        for one in plan[0]:
            one.start()
        keep.start()

    def middle():
        per_block = len(plan[1]) // len(column)
        for k, block in enumerate(column):
            arrived([block])
            for one in plan[1][k * per_block : (k + 1) * per_block]:
                one.start()

    def finish():
        per_block = len(plan[2]) // len(plane)
        for k, block in enumerate(plane):
            arrived([block])
            for one in plan[2][k * per_block : (k + 1) * per_block]:
                one.start()
        arrived(far)
        keep.wait()
        for row in plan:
            for one in row:
                one.wait_send()

    return begin, middle, finish


def backward_body(
    columns,
    height,
    fields,
    weights,
    upstream,
    out,
    everyone,
    total,
    own_sem,
    send_sems,
    recv_sems,
):
    step = pl.program_id(0)
    begin, middle, finish = gather_parts(upstream, everyone, own_sem, send_sems, recv_sems)
    pl.when(step == 0)(begin)
    pl.when(step == 4)(middle)
    place, row_tap = step // 3, step % 3
    pairs, channels = fields.shape[1], fields.shape[-1]
    source = jnp.where(place == 1, 1, 0)
    base = fields[source, :, pl.ds(2 - row_tap, height)].reshape(
        pairs * height * columns, channels
    )
    left, middle, right = column_taps(base, columns)
    term = None
    for col_tap, part in enumerate((right, middle, left)):
        product = lax.dot_general(
            part,
            weights[0, 0, col_tap],
            (((1,), (1,)), ((), ())),
            preferred_element_type=jnp.float32,
        )
        term = product if term is None else term + product
    fresh = (step == 0) | (step == 6)

    @pl.when(fresh)
    def _():
        total[...] = term

    @pl.when(jnp.logical_not(fresh))
    def _():
        total[...] += term

    def store(parity):
        value = total[...].astype(out.dtype)
        out[:, parity] = value.reshape(pairs, height * columns, channels)

    @pl.when(step == 5)
    def _():
        store(0)

    @pl.when(step == 8)
    def _():
        store(1)
        finish()


def weight_body(columns, rows, planes, upstream, out):
    cells = planes.shape[-1]
    own = planes.shape[-2]
    lane = lax.broadcasted_iota(jnp.int32, (own, cells), 1)
    column = lane % columns
    row = (lane // columns) % rows
    frame = rows * columns
    parts = []
    for time_tap in range(3):
        plane = planes[0, 0, time_tap].astype(jnp.float32)
        if time_tap < 2:
            plane = jnp.where(lane >= frame, pltpu.roll(plane, frame, 1), 0.0)
        for down in (-1, 0, 1):
            for right in (-1, 0, 1):
                shift = down * columns + right
                moved = pltpu.roll(plane, (-shift) % cells, 1) if shift else plane
                inside = (row + down >= 0) & (row + down < rows)
                inside = inside & (column + right >= 0) & (column + right < columns)
                parts.append(jnp.where(inside, moved, 0.0))
    patches = jnp.concatenate(parts, axis=0).astype(jnp.bfloat16)
    space, tm, _, _, pairs, _, _ = upstream.shape
    field = jnp.concatenate(
        [upstream[s, t, 0, 0, p] for t in range(tm) for p in range(pairs) for s in range(space)],
        axis=0,
    )
    term = jnp.dot(patches, field, preferred_element_type=jnp.float32)
    first = (pl.program_id(0) == 0) & (pl.program_id(1) == 0)

    @pl.when(first)
    def _():
        out[...] = term

    @pl.when(jnp.logical_not(first))
    def _():
        out[...] += term


def per_device(frames, clip_ids, kernel, cotangent):
    dp, tm, space = (lax.axis_size(axis) for axis in AXES)
    groups, steps, height, columns, channels = frames.shape
    pairs = clip_ids.shape[1]
    slots = groups * pairs
    frame = height * columns
    cells = slots * frame
    own = channels // (dp * tm * space)
    bf16 = jnp.bfloat16

    next_id = from_behind(clip_ids[:, :1], -1)
    prior_id = from_behind(clip_ids[:, -1:], 1)
    linked = (jnp.concatenate([prior_id, clip_ids[:, :-1]], axis=1) == clip_ids).astype(bf16)
    onward = (jnp.concatenate([clip_ids[:, 1:], next_id], axis=1) == clip_ids).astype(bf16)

    paired = frames.reshape(slots, 2, frame, channels)
    kept = onward.reshape(slots, 1, 1)
    even, odd = paired[:, 0], paired[:, 1]
    planes = jnp.stack([even * kept, odd * kept, even], axis=0).reshape(3 * cells, channels)
    sent = planes.T.reshape(dp * tm * space, own, 3 * cells)
    got = lax.all_to_all(sent, AXES, 0, 0)
    got = got.reshape(dp, tm, space, own, 3, groups, pairs, frame)
    own_planes = got.transpose(0, 5, 4, 3, 1, 6, 2, 7).reshape(dp, groups, 3, own, -1)

    rowed = row_halo(frames)
    earlier = haloed_from_behind(frames[:, -2:], 1)
    extended = jnp.concatenate([earlier, rowed], axis=1)
    gate = linked[:, :, None, None, None]
    taps = jnp.stack(
        [
            extended[:, 0 : 2 * pairs : 2] * gate,
            extended[:, 1 : 1 + 2 * pairs : 2] * gate,
            extended[:, 2 : 2 + 2 * pairs : 2],
        ],
        axis=0,
    ).reshape(3, slots, height + 2, columns, channels)

    whole = pl.BlockSpec(memory_space=pltpu.VMEM)
    params = pltpu.CompilerParams(vmem_limit_bytes=VMEM_BYTES)
    flops = 2 * 27 * cells * channels * channels
    weight_bytes = 27 * channels * channels * 2
    cost = pl.CostEstimate(flops=flops, bytes_accessed=weight_bytes, transcendentals=0)
    flat = jax.ShapeDtypeStruct((cells, channels), bf16)
    activated, upstream = pl.pallas_call(
        functools.partial(forward_body, columns, height),
        grid=(9,),
        out_shape=(flat, flat),
        in_specs=[
            whole,
            pl.BlockSpec((1, 1, 3, channels, channels), lambda i: (i // 3, i % 3, 0, 0, 0)),
            whole,
        ],
        out_specs=(
            pl.BlockSpec((cells, channels), lambda i: (0, 0)),
            pl.BlockSpec((cells, channels), lambda i: (0, 0)),
        ),
        scratch_shapes=[pltpu.VMEM((cells, channels), jnp.float32)],
        compiler_params=params,
        cost_estimate=cost,
    )(taps, kernel, cotangent.reshape(cells, channels))

    count = dp * tm * space
    grid = upstream.reshape(groups, pairs, height, columns, channels)
    padded = row_halo(grid)
    later = haloed_from_behind(grid[:, :1], -1)
    following = jnp.concatenate([padded[:, 1:], later], axis=1)
    following = following * onward[:, :, None, None, None]
    fields = jnp.stack([following, padded], axis=0).reshape(
        2, slots, height + 2, columns, channels
    )
    frame_grad, gathered = pl.pallas_call(
        functools.partial(backward_body, columns, height),
        grid=(9,),
        out_shape=(
            jax.ShapeDtypeStruct((slots, 2, frame, channels), bf16),
            jax.ShapeDtypeStruct((count, cells, channels), bf16),
        ),
        in_specs=[
            whole,
            pl.BlockSpec(
                (1, 1, 3, channels, channels), lambda i: ((i // 3) * 2 % 3, i % 3, 0, 0, 0)
            ),
            pl.BlockSpec(memory_space=pl.ANY),
        ],
        out_specs=(
            pl.BlockSpec((slots, 2, frame, channels), lambda i: (0, 0, 0, 0)),
            pl.BlockSpec(memory_space=pl.ANY),
        ),
        scratch_shapes=[
            pltpu.VMEM((cells, channels), jnp.float32),
            pltpu.SemaphoreType.DMA,
            pltpu.SemaphoreType.DMA((count - 1,)),
            pltpu.SemaphoreType.DMA((count,)),
        ],
        compiler_params=pltpu.CompilerParams(
            vmem_limit_bytes=VMEM_BYTES, collective_id=0, has_side_effects=True
        ),
        cost_estimate=cost,
    )(fields, kernel, upstream)

    per_group = gathered.reshape(space, tm, dp, groups, pairs, frame, channels)
    group_cells = tm * pairs * space * frame
    kernel_grad = pl.pallas_call(
        functools.partial(weight_body, columns, space * height),
        grid=(dp, groups),
        out_shape=jax.ShapeDtypeStruct((27 * own, channels), jnp.float32),
        in_specs=[
            pl.BlockSpec((1, 1, 3, own, group_cells), lambda a, b: (a, b, 0, 0, 0)),
            pl.BlockSpec(
                (space, tm, 1, 1, pairs, frame, channels), lambda a, b: (0, 0, a, b, 0, 0, 0)
            ),
        ],
        out_specs=pl.BlockSpec((27 * own, channels), lambda a, b: (0, 0)),
        compiler_params=params,
        cost_estimate=pl.CostEstimate(
            flops=flops, bytes_accessed=2 * gathered.size, transcendentals=0
        ),
    )(own_planes, per_group)

    return (
        activated.reshape(cotangent.shape),
        frame_grad.reshape(frames.shape),
        kernel_grad.reshape(27, own * channels),
    )


def solution(mesh):
    return jax.shard_map(
        per_device,
        mesh=mesh,
        in_specs=(
            P("dp", "tm", "space", None, None),
            P("dp", "tm"),
            P(),
            P("dp", "tm", "space", None, None),
        ),
        out_specs=(
            P("dp", "tm", "space", None, None),
            P("dp", "tm", "space", None, None),
            P(None, ("dp", "tm", "space")),
        ),
        check_vma=False,
    )
```
